256 devices in a mesh: seq: 32 (over z, y), head: 8 (over x, core).
Axes of the slice: x: 4, y: 4, z: 8, core: 2. Of those that a mesh axis runs over, the one named last changes fastest.
Arguments:
- lin_query: bfloat16 [32768, 8192], P('seq', 'head'), may hold values from -6 to 6
- lin_key: bfloat16 [32768, 8192], P('seq', 'head'), may hold values from -6 to 6
- lin_value: bfloat16 [32768, 8192], P('seq', 'head'), may hold values from -6 to 6
- log_decay: float32 [32768, 64], P('seq', 'head'), may hold values from 0 to 0.54, as said below
- norm_gain: float32 [8192], P('head'), may hold values from 0.5 to 1.5
Outputs:
- lin_out: bfloat16 [32768, 8192], P(('seq', 'head'))
The draws below stay inside these ranges and needn't reach their ends.
Inputs may be any that keep to these rules, and one draw needn't show every extreme that they name: `log_decay`: nonnegative decay exponents.
All inputs are finite; a program needn't handle non-finite values.
Results may differ from the reference program's by a relative error of at most 0.001.
Values may be sent and summed in bfloat16 or wider, within the bound.
A program may use at most 128 MiB of HBM per device.

```python
import jax
import jax.numpy as jnp
from jax import lax

HEAD_TOTAL = 64
HD = 128
SEQUENCE_TOKENS = 32768


def draw_log_decay(key, part):
    key = jax.random.fold_in(key, 11)
    key_rows = jax.random.split(key, 5)
    slow_share = 0.5
    kind_draw = jax.random.uniform(key_rows[0], (HEAD_TOTAL,))
    slow_heads = kind_draw < slow_share
    slow_rate = jax.random.uniform(key_rows[1], (HEAD_TOTAL,), minval=0.1, maxval=0.7) / SEQUENCE_TOKENS
    fast_rate = jnp.exp(jax.random.uniform(key_rows[2], (HEAD_TOTAL,), minval=jnp.log(1.0 / 50.0), maxval=jnp.log(1.0 / 30.0)))
    head_decay_rate = jnp.where(slow_heads, slow_rate, fast_rate)
    third_length = SEQUENCE_TOKENS // 3
    segment_starts = jax.random.randint(key_rows[3], (3, HEAD_TOTAL), 0, third_length) + jnp.arange(3)[:, None] * third_length
    segment_lengths = jax.random.uniform(key_rows[4], (3, HEAD_TOTAL), minval=0.22, maxval=0.5)
    token_positions = jnp.arange(SEQUENCE_TOKENS)[:, None, None] == segment_starts[None]
    token_segments = jnp.sum(jnp.where(token_positions, segment_lengths[None], 0.0), axis=1)
    return (head_decay_rate[None, :] + token_segments).astype(jnp.float32)


def steps_of(key, extent, pieces, low, largest):
    factor_of, own = 1.0, jax.random.fold_in(key, 6)
    for position, parts in pieces:
        heights = jnp.exp(jax.random.uniform(jax.random.fold_in(own, position), (parts,), jnp.float32, low / len(pieces), largest / len(pieces)))
        factor_of = factor_of * jnp.repeat(heights, extent[position] // parts).reshape([-1 if axis == position else 1 for axis in range(len(extent))])
    return factor_of


def centred(key, extent, scale, reach, shards=(), dtype=jnp.bfloat16):
    gain = steps_of(key, extent, shards, -0.22, 0.18) if shards else 1.0
    array = jax.random.normal(key, extent, jnp.float32) * scale * gain
    return jnp.minimum(jnp.maximum(array, -reach), reach).astype(dtype)


def setup_inputs(seed: int = 0) -> dict:
    key_list = jax.random.split(jax.random.key(seed), 6)
    return {
        "lin_query": centred(key_list[0], (SEQUENCE_TOKENS, HEAD_TOTAL * HD), 1.0, 6.0, ((0, 32), (1, 8))),
        "lin_key": centred(key_list[1], (SEQUENCE_TOKENS, HEAD_TOTAL * HD), 1.0, 6.0, ((0, 32), (1, 8))),
        "lin_value": centred(key_list[2], (SEQUENCE_TOKENS, HEAD_TOTAL * HD), 1.0, 6.0, ((0, 32), (1, 8))),
        "log_decay": draw_log_decay(jax.random.fold_in(key_list[5], 71), 0),
        "norm_gain": jnp.clip(1.0 + 0.1 * jax.random.normal(key_list[4], (HEAD_TOTAL * HD,), jnp.float32), 0.5, 1.5),
    }


HIGH = lax.Precision.HIGHEST

def reference(lin_query, lin_key, lin_value, log_decay, norm_gain):
    block_rows = min(128, SEQUENCE_TOKENS)
    block_count = SEQUENCE_TOKENS // block_rows
    query_heads = lin_query.reshape(block_count, block_rows, HEAD_TOTAL, HD)
    key_heads = lin_key.reshape(block_count, block_rows, HEAD_TOTAL, HD)
    value_heads = lin_value.reshape(block_count, block_rows, HEAD_TOTAL, HD)
    decay_blocks = log_decay.reshape(block_count, block_rows, HEAD_TOTAL)
    causal = jnp.arange(block_rows)[:, None] >= jnp.arange(block_rows)[None, :]

    def block_step(state, inputs):
        query_block, key_block, value_block, decay_block = inputs
        query_wide = query_block.astype(jnp.float32)
        key_wide = key_block.astype(jnp.float32)
        value_wide = value_block.astype(jnp.float32)
        cumulative = jnp.cumsum(decay_block, axis=0)
        scores = jnp.einsum('thd,shd->hts', query_wide, key_wide, precision=HIGH)
        distance = cumulative.T[:, :, None] - cumulative.T[:, None, :]
        weights = jnp.where(causal[None], jnp.exp(-jnp.maximum(distance, 0.0)), 0.0) * scores
        within = jnp.einsum('hts,shd->thd', weights, value_wide, precision=HIGH)
        carried = jnp.einsum('thd,hde->the', query_wide * jnp.exp(-cumulative)[:, :, None], state, precision=HIGH)
        ending = cumulative[-1]
        scaled_keys = key_wide * jnp.exp(-(ending[None, :] - cumulative))[:, :, None]
        updated = state * jnp.exp(-ending)[:, None, None] + jnp.einsum('shd,she->hde', scaled_keys, value_wide, precision=HIGH)
        return (updated, within + carried)
    initial = jnp.zeros((HEAD_TOTAL, HD, HD), jnp.float32)
    final_state, outputs = lax.scan(block_step, initial, (query_heads, key_heads, value_heads, decay_blocks))
    raw = outputs.reshape(SEQUENCE_TOKENS, HEAD_TOTAL, HD)
    normed = raw * lax.rsqrt(lax.optimization_barrier(jnp.mean(raw * raw, axis=-1, keepdims=True)) + 1e-06) * norm_gain.reshape(HEAD_TOTAL, HD)
    return normed.reshape(SEQUENCE_TOKENS, HEAD_TOTAL * HD).astype(jnp.bfloat16)
```

```python
import functools

import jax
import jax.numpy as jnp
from jax import lax
from jax.experimental import pallas as pl
from jax.experimental.pallas import tpu as pltpu
from jax.sharding import PartitionSpec as P

HD = 128
CHUNK = 128
MESH = pl.DeviceIdType.MESH
F32 = jnp.float32
BF16 = jnp.bfloat16
RING_Y = 4


def exact_dot(a, b):
    return jnp.dot(a, b, precision=lax.Precision.HIGHEST, preferred_element_type=F32)


def two_terms(x):
    high = x.astype(BF16)
    low = (x - high.astype(F32)).astype(BF16)
    return high, low


def wait_for(ref, sem):
    pltpu.make_async_copy(ref, ref, sem).wait()


def kernel(
    sizes,
    q_hbm, k_hbm, v_hbm, decay_hbm, gain_ref, out_hbm,
    q, k, v, decay, grow, fade, chunk_fade, start_fade, shrink,
    state, starts, inner, y_got, z_own, z_got, back, incoming, normed,
    end_y, end_z_own, end_z,
    decay_sem, q_sem, k_sem, v_sem,
    end_send, end_y_recv, end_z_recv, y_send, y_recv, z_send, z_recv, b_send, b_recv, x_send, x_recv, own_sem,
):
    heads, chunks, ny, nz = sizes
    piece = HD // ny
    seq = lax.axis_index("seq")
    head_at = lax.axis_index("head")
    my_z, my_y = seq // ny, lax.rem(seq, ny)

    def y_peer(i):
        other = lax.rem(my_y + i, ny)
        return other, {"seq": my_z * ny + other}

    def z_peer(i):
        other = lax.rem(my_z + i, nz)
        return other, {"seq": other * ny + my_y}

    def x_peer(i):
        other = lax.rem(head_at + i, chunks)
        return other, {"head": other}

    def remote(src, dst, send, recv, device):
        return pltpu.make_async_remote_copy(src, dst, send, recv, device_id=device, device_id_type=MESH)

    def columns(h):
        return pl.ds(pl.multiple_of(h * HD, HD), HD)

    def load(array_hbm, array, sems, h):
        return pltpu.make_async_copy(array_hbm.at[:, columns(h)], array.at[h], sems.at[h])

    decay_copy = pltpu.make_async_copy(decay_hbm, decay, decay_sem)
    decay_copy.start()
    barrier = pltpu.get_barrier_semaphore()
    for i in range(1, ny):
        pl.semaphore_signal(barrier, inc=1, device_id=y_peer(i)[1], device_id_type=MESH)
    for i in range(1, nz):
        pl.semaphore_signal(barrier, inc=1, device_id=z_peer(i)[1], device_id_type=MESH)
    for i in range(1, chunks):
        pl.semaphore_signal(barrier, inc=1, device_id=x_peer(i)[1], device_id_type=MESH)

    @pl.loop(0, heads)
    def _(h):
        load(k_hbm, k, k_sem, h).start()
        load(v_hbm, v, v_sem, h).start()

    @pl.loop(0, heads)
    def _(h):
        load(q_hbm, q, q_sem, h).start()

    decay_copy.wait()
    row = lax.broadcasted_iota(jnp.int32, (CHUNK, CHUNK), 0)
    col = lax.broadcasted_iota(jnp.int32, (CHUNK, CHUNK), 1)
    rates = jnp.concatenate([decay[j * CHUNK : (j + 1) * CHUNK, :].T for j in range(chunks)], axis=0)
    cumulative = exact_dot(rates, (row <= col).astype(F32))
    ending = exact_dot(rates, jnp.ones((CHUNK, CHUNK), F32))
    grow[...] = jnp.exp(cumulative)
    fade[...] = jnp.exp(cumulative - ending)
    chunk_fade[...] = jnp.exp(-ending)
    so_far = jnp.zeros((heads, HD), F32)
    for j in range(chunks):
        start_fade[j * heads : (j + 1) * heads, :] = jnp.exp(-so_far)
        so_far = so_far + ending[j * heads : (j + 1) * heads, :]
    end_y[my_y] = so_far
    shrink[...] = jnp.exp(-cumulative).T

    def local_state(h):
        load(k_hbm, k, k_sem, h).wait()
        load(v_hbm, v, v_sem, h).wait()
        total = jnp.zeros((HD, HD), F32)
        for j in range(chunks):
            rows = slice(j * CHUNK, (j + 1) * CHUNK)
            at = pl.ds(j * heads + h, 1)
            starts[h, j, 0:HD, :], starts[h, j, HD : 2 * HD, :] = two_terms(total)
            keys = k[h, rows, :].astype(F32).T * fade[at, :]
            values = v[h, rows, :]
            added = jnp.dot(
                jnp.concatenate(two_terms(keys), axis=1),
                jnp.concatenate([values, values], axis=0),
                preferred_element_type=F32,
            )
            total = total * chunk_fade[at, :] + added
        state[h] = total
        y_got[h, my_y] = state[h, pl.ds(pl.multiple_of(my_y * piece, piece), piece), :]

    def send_y(h):
        for i in range(1, ny):
            other, device = y_peer(i)
            rows = pl.ds(pl.multiple_of(other * piece, piece), piece)
            remote(state.at[h, rows], y_got.at[h, my_y], y_send, y_recv.at[h], device).start()

    def group_total(h):
        wait_for(y_got.at[h, pl.ds(0, ny - 1)], y_recv.at[h])
        total = y_got[h, 0]
        for y in range(1, ny):
            total = total * jnp.exp(-end_y[y, pl.ds(h, 1), :]) + y_got[h, y]
        z_own[h] = total
        z_got[h, my_z] = total
        for i in range(1, nz):
            device = z_peer(i)[1]
            remote(z_own.at[h], z_got.at[h, my_z], z_send, z_recv.at[h], device).start()

    def hand_back(h):
        wait_for(z_got.at[h, pl.ds(0, nz - 1)], z_recv.at[h])

        def add(z, total):
            return total * jnp.exp(-end_z[z, pl.ds(h, 1), :]) + z_got[h, z]

        total = lax.fori_loop(0, my_z, add, jnp.zeros((piece, HD), F32))
        for y in range(ny):
            back[h, y] = total
            if y + 1 < ny:
                total = total * jnp.exp(-end_y[y, pl.ds(h, 1), :]) + y_got[h, y]
        mine = pl.ds(pl.multiple_of(my_y * piece, piece), piece)
        incoming[h, mine, :] = back[h, my_y]
        for i in range(1, ny):
            other, device = y_peer(i)
            remote(back.at[h, other], incoming.at[h, mine], b_send, b_recv.at[h], device).start()

    def within(h):
        load(q_hbm, q, q_sem, h).wait()
        causal = row >= col
        for j in range(chunks):
            rows = slice(j * CHUNK, (j + 1) * CHUNK)
            at = pl.ds(j * heads + h, 1)
            queries, keys, values = q[h, rows, :], k[h, rows, :], v[h, rows, :]
            scores = lax.dot_general(queries, keys, (((1,), (1,)), ((), ())), preferred_element_type=F32)
            weights = jnp.where(causal, scores * grow[at, :], 0.0)
            inner[h, rows, :] = jnp.dot(
                jnp.concatenate(two_terms(weights), axis=1),
                jnp.concatenate([values, values], axis=0),
                preferred_element_type=F32,
            ) + jnp.dot(
                jnp.concatenate([queries, queries], axis=1), starts[h, j], preferred_element_type=F32
            )

    def finish(h):
        wait_for(incoming.at[h, pl.ds(0, (ny - 1) * piece)], b_recv.at[h])
        entering = jnp.concatenate(two_terms(incoming[h]), axis=0)
        gain = gain_ref[pl.ds(h, 1), :]
        target = pl.ds(pl.multiple_of((head_at * heads + h) * HD, HD), HD)
        lane = lax.broadcasted_iota(jnp.int32, (CHUNK, chunks * heads), 1)
        for i in range(1, chunks + 1):
            j, device = x_peer(i)
            rows = pl.ds(pl.multiple_of(j * CHUNK, CHUNK), CHUNK)
            at = j * heads + h
            queries = q[h, rows, :]
            carried = jnp.dot(
                jnp.concatenate([queries, queries], axis=1), entering, preferred_element_type=F32
            )
            scale = jnp.sum(jnp.where(lane == at, shrink[...], 0.0), axis=1, keepdims=True)
            raw = (inner[h, rows, :] + carried * start_fade[pl.ds(at, 1), :]) * scale
            square = jnp.mean(raw * raw, axis=1, keepdims=True)
            normed[h, j] = (raw * lax.rsqrt(square + 1e-06) * gain).astype(BF16)
            if i < chunks:
                remote(normed.at[h, j], out_hbm.at[:, target], x_send, x_recv, device).start()
            else:
                pltpu.make_async_copy(normed.at[h, j], out_hbm.at[:, target], own_sem.at[h]).start()

    local_state(0)
    pl.semaphore_wait(barrier, ny + nz + chunks - 3)
    for i in range(1, ny):
        remote(end_y.at[my_y], end_y.at[my_y], end_send, end_y_recv, y_peer(i)[1]).start()
    send_y(0)

    @pl.loop(1, heads)
    def _(h):
        local_state(h)
        send_y(h)

    wait_for(end_y.at[pl.ds(0, ny - 1)], end_y_recv)
    group_end = end_y[0]
    for y in range(1, ny):
        group_end = group_end + end_y[y]
    end_z_own[...] = group_end
    end_z[my_z] = group_end
    for i in range(1, nz):
        remote(end_z_own, end_z.at[my_z], end_send, end_z_recv, z_peer(i)[1]).start()

    @pl.loop(0, heads)
    def _(h):
        group_total(h)

    within(0)
    wait_for(end_z.at[pl.ds(0, nz - 1)], end_z_recv)
    hand_back(0)

    @pl.loop(1, heads)
    def _(h):
        within(h)
        hand_back(h)
        finish(h - 1)

    finish(heads - 1)

    wait_for(end_y.at[pl.ds(0, ny - 1)], end_send)
    wait_for(end_z.at[pl.ds(0, nz - 1)], end_send)

    @pl.loop(0, heads)
    def _(h):
        wait_for(y_got.at[h, pl.ds(0, ny - 1)], y_send)
        wait_for(z_got.at[h, pl.ds(0, nz - 1)], z_send)
        wait_for(back.at[h, pl.ds(0, ny - 1)], b_send)
        wait_for(normed.at[h, pl.ds(0, chunks - 1)], x_send)
        target = pl.ds(pl.multiple_of((head_at * heads + h) * HD, HD), HD)
        pltpu.make_async_copy(normed.at[h, head_at], out_hbm.at[:, target], own_sem.at[h]).wait()

    wait_for(out_hbm.at[:, pl.ds(0, (chunks - 1) * heads * HD)], x_recv)


def on_device(lin_query, lin_key, lin_value, log_decay, norm_gain):
    tokens, width = lin_query.shape
    heads, chunks = width // HD, tokens // CHUNK
    ny = RING_Y
    nz = lax.axis_size("seq") // ny
    piece = HD // ny
    rows = chunks * heads
    any_space = pl.BlockSpec(memory_space=pl.ANY)
    dma = pltpu.SemaphoreType.DMA
    return pl.pallas_call(
        functools.partial(kernel, (heads, chunks, ny, nz)),
        out_shape=jax.ShapeDtypeStruct((CHUNK, chunks * width), BF16),
        in_specs=[any_space] * 4 + [pl.BlockSpec(memory_space=pltpu.VMEM)],
        out_specs=any_space,
        scratch_shapes=[
            pltpu.VMEM((heads, tokens, HD), BF16),
            pltpu.VMEM((heads, tokens, HD), BF16),
            pltpu.VMEM((heads, tokens, HD), BF16),
            pltpu.VMEM((tokens, heads), F32),
            pltpu.VMEM((rows, CHUNK), F32),
            pltpu.VMEM((rows, CHUNK), F32),
            pltpu.VMEM((rows, CHUNK), F32),
            pltpu.VMEM((rows, CHUNK), F32),
            pltpu.VMEM((CHUNK, rows), F32),
            pltpu.VMEM((heads, HD, HD), F32),
            pltpu.VMEM((heads, chunks, 2 * HD, HD), BF16),
            pltpu.VMEM((heads, tokens, HD), F32),
            pltpu.VMEM((heads, ny, piece, HD), F32),
            pltpu.VMEM((heads, piece, HD), F32),
            pltpu.VMEM((heads, nz, piece, HD), F32),
            pltpu.VMEM((heads, ny, piece, HD), F32),
            pltpu.VMEM((heads, HD, HD), F32),
            pltpu.VMEM((heads, chunks, CHUNK, HD), BF16),
            pltpu.VMEM((ny, heads, HD), F32),
            pltpu.VMEM((heads, HD), F32),
            pltpu.VMEM((nz, heads, HD), F32),
            dma, dma((heads,)), dma((heads,)), dma((heads,)),
            dma, dma, dma, dma, dma((heads,)), dma, dma((heads,)), dma, dma((heads,)), dma, dma,
            dma((heads,)),
        ],
        compiler_params=pltpu.CompilerParams(
            collective_id=0, has_side_effects=True, vmem_limit_bytes=52 * 2**20
        ),
        name="lightning",
    )(lin_query, lin_key, lin_value, log_decay, norm_gain.reshape(heads, HD))


def solution(mesh):
    in_specs = (P("seq", "head"), P("seq", "head"), P("seq", "head"), P("seq", "head"), P("head"))
    out_specs = P(("seq", "head"), None)
    return jax.shard_map(
        on_device, mesh=mesh, in_specs=in_specs, out_specs=out_specs, check_vma=False
    )
```

```python
import functools

import jax
import jax.numpy as jnp
from jax import lax
from jax.experimental import pallas as pl
from jax.experimental.pallas import tpu as pltpu
from jax.sharding import PartitionSpec as P

HD = 128
CHUNK = 128
MESH = pl.DeviceIdType.MESH
F32 = jnp.float32
BF16 = jnp.bfloat16
RING_Y = 4
DIRECT = 4


def exact_dot(a, b):
    return jnp.dot(a, b, precision=lax.Precision.HIGHEST, preferred_element_type=F32)


def two_terms(x):
    high = x.astype(BF16)
    low = (x - high.astype(F32)).astype(BF16)
    return high, low


def wait_for(ref, sem):
    pltpu.make_async_copy(ref, ref, sem).wait()


def kernel(
    sizes,
    q_hbm, k_hbm, v_hbm, decay_hbm, gain_hbm, out_hbm,
    q, k, v, decay, gains, grow, fade, chunk_fade, start_fade, shrink,
    state, starts, inner, y_got, z_own, z_got, back, incoming, normed,
    group, group_got, group_back, group_in,
    end_y, end_z_own, end_z,
    decay_sem, gain_sem, q_sem, k_sem, v_sem,
    end_send, end_y_recv, end_z_recv, y_send, y_recv, z_send, z_recv, b_send, b_recv, x_send, x_recv, own_sem,
    g_send, g_recv, gb_send, gb_recv,
):
    heads, chunks, ny, nz = sizes
    piece = HD // ny
    share = (heads - DIRECT) * piece // nz
    seq = lax.axis_index("seq")
    head_at = lax.axis_index("head")
    my_z, my_y = seq // ny, lax.rem(seq, ny)

    def y_peer(i):
        other = lax.rem(my_y + i, ny)
        return other, {"seq": my_z * ny + other}

    def z_peer(i):
        other = lax.rem(my_z + i, nz)
        return other, {"seq": other * ny + my_y}

    def x_peer(i):
        other = lax.rem(head_at + i, chunks)
        return other, {"head": other}

    def remote(src, dst, send, recv, device):
        return pltpu.make_async_remote_copy(src, dst, send, recv, device_id=device, device_id_type=MESH)

    def columns(h):
        return pl.ds(pl.multiple_of(h * HD, HD), HD)

    decay_copy = pltpu.make_async_copy(decay_hbm, decay, decay_sem)
    decay_copy.start()
    gain_copy = pltpu.make_async_copy(gain_hbm, gains, gain_sem)
    gain_copy.start()
    k_copy = pltpu.make_async_copy(k_hbm, k, k_sem)
    k_copy.start()
    v_copy = pltpu.make_async_copy(v_hbm, v, v_sem)
    v_copy.start()
    q_copy = pltpu.make_async_copy(q_hbm, q, q_sem)
    q_copy.start()
    barrier = pltpu.get_barrier_semaphore()
    for i in range(1, ny):
        pl.semaphore_signal(barrier, inc=1, device_id=y_peer(i)[1], device_id_type=MESH)
    for i in range(1, nz):
        pl.semaphore_signal(barrier, inc=1, device_id=z_peer(i)[1], device_id_type=MESH)
    for i in range(1, chunks):
        pl.semaphore_signal(barrier, inc=1, device_id=x_peer(i)[1], device_id_type=MESH)

    decay_copy.wait()
    row = lax.broadcasted_iota(jnp.int32, (CHUNK, CHUNK), 0)
    col = lax.broadcasted_iota(jnp.int32, (CHUNK, CHUNK), 1)
    rates = jnp.concatenate([decay[:, j * CHUNK : (j + 1) * CHUNK] for j in range(chunks)], axis=0)
    cumulative = exact_dot(rates, (row <= col).astype(F32))
    ending = exact_dot(rates, jnp.ones((CHUNK, CHUNK), F32))
    grow[...] = jnp.exp(cumulative)
    fade[...] = jnp.exp(cumulative - ending)
    chunk_fade[...] = jnp.exp(-ending)
    so_far = jnp.zeros((heads, HD), F32)
    for j in range(chunks):
        start_fade[j * heads : (j + 1) * heads, :] = jnp.exp(-so_far)
        so_far = so_far + ending[j * heads : (j + 1) * heads, :]
    end_y[my_y] = so_far
    shrink[...] = jnp.exp(-cumulative).T

    def local_state(h):
        total = jnp.zeros((HD, HD), F32)
        for j in range(chunks):
            rows = slice(j * CHUNK, (j + 1) * CHUNK)
            at = pl.ds(j * heads + h, 1)
            starts[h, j, 0:HD, :], starts[h, j, HD : 2 * HD, :] = two_terms(total)
            keys = k[rows, columns(h)].astype(F32).T * fade[at, :]
            values = v[rows, columns(h)]
            added = jnp.dot(
                jnp.concatenate(two_terms(keys), axis=1),
                jnp.concatenate([values, values], axis=0),
                preferred_element_type=F32,
            )
            total = total * chunk_fade[at, :] + added
        state[h] = total
        y_got[h, my_y] = state[h, pl.ds(pl.multiple_of(my_y * piece, piece), piece), :]

    def send_y(h):
        for i in range(1, ny):
            other, device = y_peer(i)
            rows = pl.ds(pl.multiple_of(other * piece, piece), piece)
            remote(state.at[h, rows], y_got.at[h, my_y], y_send, y_recv.at[h], device).start()

    def group_total(h):
        wait_for(y_got.at[h, pl.ds(0, ny - 1)], y_recv.at[h])
        total = y_got[h, 0]
        for y in range(1, ny):
            total = total * jnp.exp(-end_y[y, pl.ds(h, 1), :]) + y_got[h, y]
        return total

    def send_z(h):
        total = group_total(h)
        z_own[h] = total
        z_got[h, my_z] = total
        for i in range(1, nz):
            device = z_peer(i)[1]
            remote(z_own.at[h], z_got.at[h, my_z], z_send.at[h], z_recv.at[h], device).start()

    def z_sent(h):
        wait_for(z_got.at[h, pl.ds(0, nz - 1)], z_send.at[h])

    def group_rows(z):
        return pl.ds(pl.multiple_of(z * share, share), share)

    def send_group():
        group_got[my_z] = group[group_rows(my_z), :]
        for i in range(1, nz):
            other, device = z_peer(i)
            remote(group.at[group_rows(other)], group_got.at[my_z], g_send, g_recv, device).start()

    def scan_group():
        wait_for(group_got.at[pl.ds(0, nz - 1)], g_recv)
        h = DIRECT + (my_z * share) // piece
        total = jnp.zeros((share, HD), F32)
        for z in range(nz):
            group_back[z] = total
            if z + 1 < nz:
                total = total * jnp.exp(-end_z[z, pl.ds(h, 1), :]) + group_got[z]
        mine = group_rows(my_z)
        group_in[mine, :] = group_back[my_z]
        for i in range(1, nz):
            other, device = z_peer(i)
            remote(group_back.at[other], group_in.at[mine], gb_send, gb_recv, device).start()

    def direct_before(h):
        wait_for(z_got.at[h, pl.ds(0, nz - 1)], z_recv.at[h])

        def add(z, total):
            return total * jnp.exp(-end_z[z, pl.ds(h, 1), :]) + z_got[h, z]

        return lax.fori_loop(0, my_z, add, jnp.zeros((piece, HD), F32))

    def group_before(h):
        return group_in[pl.ds(pl.multiple_of((h - DIRECT) * piece, piece), piece), :]

    def hand_back(h, total):
        for y in range(ny):
            back[h, y] = total
            if y + 1 < ny:
                total = total * jnp.exp(-end_y[y, pl.ds(h, 1), :]) + y_got[h, y]
        mine = pl.ds(pl.multiple_of(my_y * piece, piece), piece)
        incoming[h, mine, :] = back[h, my_y]
        for i in range(1, ny):
            other, device = y_peer(i)
            remote(back.at[h, other], incoming.at[h, mine], b_send, b_recv.at[h], device).start()

    def within(h):
        causal = row >= col
        for j in range(chunks):
            rows = slice(j * CHUNK, (j + 1) * CHUNK)
            at = pl.ds(j * heads + h, 1)
            queries, keys, values = q[rows, columns(h)], k[rows, columns(h)], v[rows, columns(h)]
            scores = lax.dot_general(queries, keys, (((1,), (1,)), ((), ())), preferred_element_type=F32)
            weights = jnp.where(causal, scores * grow[at, :], 0.0)
            inner[h, rows, :] = jnp.dot(
                jnp.concatenate(two_terms(weights), axis=1),
                jnp.concatenate([values, values], axis=0),
                preferred_element_type=F32,
            ) + jnp.dot(
                jnp.concatenate([queries, queries], axis=1), starts[h, j], preferred_element_type=F32
            )

    def finish(h):
        wait_for(incoming.at[h, pl.ds(0, (ny - 1) * piece)], b_recv.at[h])
        entering = jnp.concatenate(two_terms(incoming[h]), axis=0)
        gain = gains[pl.ds(h, 1), :]
        target = pl.ds(pl.multiple_of((head_at * heads + h) * HD, HD), HD)
        lane = lax.broadcasted_iota(jnp.int32, (CHUNK, chunks * heads), 1)
        for i in range(1, chunks + 1):
            j, device = x_peer(i)
            rows = pl.ds(pl.multiple_of(j * CHUNK, CHUNK), CHUNK)
            at = j * heads + h
            queries = q[rows, columns(h)]
            carried = jnp.dot(
                jnp.concatenate([queries, queries], axis=1), entering, preferred_element_type=F32
            )
            scale = jnp.sum(jnp.where(lane == at, shrink[...], 0.0), axis=1, keepdims=True)
            raw = (inner[h, rows, :] + carried * start_fade[pl.ds(at, 1), :]) * scale
            square = jnp.mean(raw * raw, axis=1, keepdims=True)
            normed[h, j] = (raw * lax.rsqrt(square + 1e-06) * gain).astype(BF16)
            if i < chunks:
                remote(normed.at[h, j], out_hbm.at[:, target], x_send, x_recv, device).start()
            else:
                pltpu.make_async_copy(normed.at[h, j], out_hbm.at[:, target], own_sem.at[h]).start()

    k_copy.wait()
    v_copy.wait()
    local_state(0)
    pl.semaphore_wait(barrier, ny + nz + chunks - 3)
    for i in range(1, ny):
        remote(end_y.at[my_y], end_y.at[my_y], end_send, end_y_recv, y_peer(i)[1]).start()
    send_y(0)

    @pl.loop(1, DIRECT)
    def _(h):
        local_state(h)
        send_y(h)

    wait_for(end_y.at[pl.ds(0, ny - 1)], end_y_recv)
    group_end = end_y[0]
    for y in range(1, ny):
        group_end = group_end + end_y[y]
    end_z_own[...] = group_end
    end_z[my_z] = group_end
    for i in range(1, nz):
        remote(end_z_own, end_z.at[my_z], end_send, end_z_recv, z_peer(i)[1]).start()
    send_z(0)

    @pl.loop(DIRECT, heads)
    def _(h):
        local_state(h)
        send_y(h)

    z_sent(0)
    send_z(1)

    @pl.loop(DIRECT, heads)
    def _(h):
        group[pl.ds(pl.multiple_of((h - DIRECT) * piece, piece), piece), :] = group_total(h)

    send_group()
    q_copy.wait()
    within(0)
    z_sent(1)
    send_z(2)
    within(1)
    gain_copy.wait()
    wait_for(end_z.at[pl.ds(0, nz - 1)], end_z_recv)
    hand_back(0, direct_before(0))
    z_sent(2)
    send_z(3)
    within(2)
    hand_back(1, direct_before(1))
    finish(0)
    scan_group()

    @pl.loop(2, DIRECT)
    def _(h):
        within(h + 1)
        hand_back(h, direct_before(h))
        finish(h - 1)

    wait_for(group_in.at[pl.ds(0, (nz - 1) * share)], gb_recv)

    @pl.loop(DIRECT, heads)
    def _(h):
        hand_back(h, group_before(h))

    @pl.loop(DIRECT, heads)
    def _(h):
        finish(h - 1)

        @pl.when(h + 1 < heads)
        def _():
            within(h + 1)

    finish(heads - 1)

    wait_for(end_y.at[pl.ds(0, ny - 1)], end_send)
    wait_for(end_z.at[pl.ds(0, nz - 1)], end_send)
    wait_for(group_got.at[pl.ds(0, nz - 1)], g_send)
    wait_for(group_got.at[pl.ds(0, nz - 1)], gb_send)

    z_sent(DIRECT - 1)

    @pl.loop(0, heads)
    def _(h):
        wait_for(y_got.at[h, pl.ds(0, ny - 1)], y_send)
        wait_for(back.at[h, pl.ds(0, ny - 1)], b_send)
        wait_for(normed.at[h, pl.ds(0, chunks - 1)], x_send)
        target = pl.ds(pl.multiple_of((head_at * heads + h) * HD, HD), HD)
        pltpu.make_async_copy(normed.at[h, head_at], out_hbm.at[:, target], own_sem.at[h]).wait()

    wait_for(out_hbm.at[:, pl.ds(0, (chunks - 1) * heads * HD)], x_recv)


def on_device(lin_query, lin_key, lin_value, log_decay, norm_gain):
    tokens, width = lin_query.shape
    heads, chunks = width // HD, tokens // CHUNK
    ny = RING_Y
    nz = lax.axis_size("seq") // ny
    piece = HD // ny
    rows = chunks * heads
    share = (heads - DIRECT) * piece // nz
    in_hbm = pl.BlockSpec(memory_space=pltpu.HBM)
    dma = pltpu.SemaphoreType.DMA
    return pl.pallas_call(
        functools.partial(kernel, (heads, chunks, ny, nz)),
        out_shape=pltpu.VMEM((CHUNK, chunks * width), BF16),
        in_specs=[in_hbm] * 5,
        out_specs=pl.BlockSpec(memory_space=pltpu.VMEM),
        scratch_shapes=[
            pltpu.VMEM((tokens, width), BF16),
            pltpu.VMEM((tokens, width), BF16),
            pltpu.VMEM((tokens, width), BF16),
            pltpu.VMEM((heads, tokens), F32),
            pltpu.VMEM((heads, HD), F32),
            pltpu.VMEM((rows, CHUNK), F32),
            pltpu.VMEM((rows, CHUNK), F32),
            pltpu.VMEM((rows, CHUNK), F32),
            pltpu.VMEM((rows, CHUNK), F32),
            pltpu.VMEM((CHUNK, rows), F32),
            pltpu.VMEM((heads, HD, HD), F32),
            pltpu.VMEM((heads, chunks, 2 * HD, HD), BF16),
            pltpu.VMEM((heads, tokens, HD), F32),
            pltpu.VMEM((heads, ny, piece, HD), F32),
            pltpu.VMEM((DIRECT, piece, HD), F32),
            pltpu.VMEM((DIRECT, nz, piece, HD), F32),
            pltpu.VMEM((heads, ny, piece, HD), F32),
            pltpu.VMEM((heads, HD, HD), F32),
            pltpu.VMEM((heads, chunks, CHUNK, HD), BF16),
            pltpu.VMEM((nz * share, HD), F32),
            pltpu.VMEM((nz, share, HD), F32),
            pltpu.VMEM((nz, share, HD), F32),
            pltpu.VMEM((nz * share, HD), F32),
            pltpu.VMEM((ny, heads, HD), F32),
            pltpu.VMEM((heads, HD), F32),
            pltpu.VMEM((nz, heads, HD), F32),
            dma, dma, dma, dma, dma,
            dma, dma, dma, dma, dma((heads,)), dma((DIRECT,)), dma((DIRECT,)), dma, dma((heads,)), dma, dma,
            dma((heads,)), dma, dma, dma, dma,
        ],
        compiler_params=pltpu.CompilerParams(
            collective_id=0, has_side_effects=True, vmem_limit_bytes=60 * 2**20
        ),
        name="lightning",
    )(lin_query, lin_key, lin_value, log_decay.T, norm_gain.reshape(heads, HD))


def solution(mesh):
    in_specs = (P("seq", "head"), P("seq", "head"), P("seq", "head"), P("seq", "head"), P("head"))
    out_specs = P(("seq", "head"), None)
    return jax.shard_map(
        on_device, mesh=mesh, in_specs=in_specs, out_specs=out_specs, check_vma=False
    )
```

```python
import functools

import jax
import jax.numpy as jnp
from jax import lax
from jax.experimental import pallas as pl
from jax.experimental.pallas import tpu as pltpu
from jax.sharding import PartitionSpec as P

HD = 128
CHUNK = 128
MESH = pl.DeviceIdType.MESH
F32 = jnp.float32
BF16 = jnp.bfloat16
RING_Y = 4
DIRECT = 4


def exact_dot(a, b):
    return jnp.dot(a, b, precision=lax.Precision.HIGHEST, preferred_element_type=F32)


def two_terms(x):
    high = x.astype(BF16)
    low = (x - high.astype(F32)).astype(BF16)
    return high, low


def wait_for(ref, sem):
    pltpu.make_async_copy(ref, ref, sem).wait()


def kernel(
    sizes,
    q_hbm, k_hbm, v_hbm, decay_hbm, gain_hbm, out_hbm,
    q, k, v, decay, gains, grow, fade, chunk_fade, start_fade, shrink,
    state, starts, inner, y_got, z_own, z_got, back, incoming, normed,
    group, group_got, group_back, group_in,
    end_y, end_z_own, end_z,
    decay_sem, gain_sem, q_sem, k_sem, v_sem,
    end_send, end_y_recv, end_z_recv, y_send, y_recv, z_send, z_recv, b_send, b_recv, x_send, x_recv, own_sem,
    g_send, g_recv, gb_send, gb_recv,
):
    heads, chunks, ny, nz = sizes
    piece = HD // ny
    share = (heads - DIRECT) * piece // nz
    seq = lax.axis_index("seq")
    head_at = lax.axis_index("head")
    my_z, my_y = seq // ny, lax.rem(seq, ny)

    def y_peer(i):
        other = lax.rem(my_y + i, ny)
        return other, {"seq": my_z * ny + other}

    def z_peer(i):
        other = lax.rem(my_z + i, nz)
        return other, {"seq": other * ny + my_y}

    def x_peer(i):
        other = lax.rem(head_at + i, chunks)
        return other, {"head": other}

    def remote(src, dst, send, recv, device):
        return pltpu.make_async_remote_copy(src, dst, send, recv, device_id=device, device_id_type=MESH)

    def columns(h):
        return pl.ds(pl.multiple_of(h * HD, HD), HD)

    decay_copy = pltpu.make_async_copy(decay_hbm, decay, decay_sem)
    decay_copy.start()
    gain_copy = pltpu.make_async_copy(gain_hbm, gains, gain_sem)
    gain_copy.start()
    k_copy = pltpu.make_async_copy(k_hbm, k, k_sem)
    k_copy.start()
    v_copy = pltpu.make_async_copy(v_hbm, v, v_sem)
    v_copy.start()
    q_copy = pltpu.make_async_copy(q_hbm, q, q_sem)
    barrier = pltpu.get_barrier_semaphore()
    for i in range(1, ny):
        pl.semaphore_signal(barrier, inc=1, device_id=y_peer(i)[1], device_id_type=MESH)
    for i in range(1, nz):
        pl.semaphore_signal(barrier, inc=1, device_id=z_peer(i)[1], device_id_type=MESH)
    for i in range(1, chunks):
        pl.semaphore_signal(barrier, inc=1, device_id=x_peer(i)[1], device_id_type=MESH)

    decay_copy.wait()
    row = lax.broadcasted_iota(jnp.int32, (CHUNK, CHUNK), 0)
    col = lax.broadcasted_iota(jnp.int32, (CHUNK, CHUNK), 1)
    rates = jnp.concatenate([decay[:, j * CHUNK : (j + 1) * CHUNK] for j in range(chunks)], axis=0)
    cumulative = exact_dot(rates, (row <= col).astype(F32))
    ending = jnp.broadcast_to(cumulative[:, CHUNK - 1 :], cumulative.shape)
    fade[...] = jnp.exp(cumulative - ending)
    chunk_fade[...] = jnp.exp(-ending)
    so_far = jnp.zeros((heads, HD), F32)
    for j in range(chunks):
        start_fade[j * heads : (j + 1) * heads, :] = so_far
        so_far = so_far + ending[j * heads : (j + 1) * heads, :]
    end_y[my_y] = so_far
    grow[...] = cumulative

    def local_state(h):
        total = jnp.zeros((HD, HD), F32)
        for j in range(chunks):
            rows = slice(j * CHUNK, (j + 1) * CHUNK)
            at = pl.ds(j * heads + h, 1)
            starts[h, j, 0:HD, :], starts[h, j, HD : 2 * HD, :] = two_terms(total)
            keys = k[rows, columns(h)].astype(F32).T * fade[at, :]
            values = v[rows, columns(h)]
            added = jnp.dot(
                jnp.concatenate(two_terms(keys), axis=1),
                jnp.concatenate([values, values], axis=0),
                preferred_element_type=F32,
            )
            total = total * chunk_fade[at, :] + added
        state[h] = total
        y_got[h, my_y] = state[h, pl.ds(pl.multiple_of(my_y * piece, piece), piece), :]

    def send_y(h):
        for i in range(1, ny):
            other, device = y_peer(i)
            rows = pl.ds(pl.multiple_of(other * piece, piece), piece)
            remote(state.at[h, rows], y_got.at[h, my_y], y_send, y_recv.at[h], device).start()

    def group_total(h):
        wait_for(y_got.at[h, pl.ds(0, ny - 1)], y_recv.at[h])
        total = y_got[h, 0]
        for y in range(1, ny):
            total = total * jnp.exp(-end_y[y, pl.ds(h, 1), :]) + y_got[h, y]
        return total

    def send_z(h):
        total = group_total(h)
        z_own[h] = total
        z_got[h, my_z] = total
        for i in range(1, nz):
            device = z_peer(i)[1]
            remote(z_own.at[h], z_got.at[h, my_z], z_send.at[h], z_recv.at[h], device).start()

    def z_sent(h):
        wait_for(z_got.at[h, pl.ds(0, nz - 1)], z_send.at[h])

    def group_rows(z):
        return pl.ds(pl.multiple_of(z * share, share), share)

    def send_group():
        group_got[my_z] = group[group_rows(my_z), :]
        for i in range(1, nz):
            other, device = z_peer(i)
            remote(group.at[group_rows(other)], group_got.at[my_z], g_send, g_recv, device).start()

    def scan_group():
        wait_for(group_got.at[pl.ds(0, nz - 1)], g_recv)
        h = DIRECT + (my_z * share) // piece
        total = jnp.zeros((share, HD), F32)
        for z in range(nz):
            group_back[z] = total
            if z + 1 < nz:
                total = total * jnp.exp(-end_z[z, pl.ds(h, 1), :]) + group_got[z]
        mine = group_rows(my_z)
        group_in[mine, :] = group_back[my_z]
        for i in range(1, nz):
            other, device = z_peer(i)
            remote(group_back.at[other], group_in.at[mine], gb_send, gb_recv, device).start()

    def direct_before(h):
        wait_for(z_got.at[h, pl.ds(0, nz - 1)], z_recv.at[h])

        def add(z, total):
            return total * jnp.exp(-end_z[z, pl.ds(h, 1), :]) + z_got[h, z]

        return lax.fori_loop(0, my_z, add, jnp.zeros((piece, HD), F32))

    def group_before(h):
        return group_in[pl.ds(pl.multiple_of((h - DIRECT) * piece, piece), piece), :]

    def hand_back(h, total):
        for y in range(ny):
            back[h, y] = total
            if y + 1 < ny:
                total = total * jnp.exp(-end_y[y, pl.ds(h, 1), :]) + y_got[h, y]
        mine = pl.ds(pl.multiple_of(my_y * piece, piece), piece)
        incoming[h, mine, :] = back[h, my_y]
        for i in range(1, ny):
            other, device = y_peer(i)
            remote(back.at[h, other], incoming.at[h, mine], b_send, b_recv.at[h], device).start()

    def within(h):
        causal = row >= col
        for j in range(chunks):
            rows = slice(j * CHUNK, (j + 1) * CHUNK)
            at = pl.ds(j * heads + h, 1)
            queries, keys, values = q[rows, columns(h)], k[rows, columns(h)], v[rows, columns(h)]
            scores = lax.dot_general(queries, keys, (((1,), (1,)), ((), ())), preferred_element_type=F32)
            weights = jnp.where(causal, scores * grow[at, :], 0.0)
            inner[h, rows, :] = jnp.dot(
                jnp.concatenate(two_terms(weights), axis=1),
                jnp.concatenate([values, values], axis=0),
                preferred_element_type=F32,
            ) + jnp.dot(
                jnp.concatenate([queries, queries], axis=1), starts[h, j], preferred_element_type=F32
            )

    def finish(h):
        wait_for(incoming.at[h, pl.ds(0, (ny - 1) * piece)], b_recv.at[h])
        entering = jnp.concatenate(two_terms(incoming[h]), axis=0)
        gain = gains[pl.ds(h, 1), :]
        target = pl.ds(pl.multiple_of((head_at * heads + h) * HD, HD), HD)
        lane = lax.broadcasted_iota(jnp.int32, (CHUNK, chunks * heads), 1)
        for i in range(1, chunks + 1):
            j, device = x_peer(i)
            rows = pl.ds(pl.multiple_of(j * CHUNK, CHUNK), CHUNK)
            at = j * heads + h
            queries = q[rows, columns(h)]
            carried = jnp.dot(
                jnp.concatenate([queries, queries], axis=1), entering, preferred_element_type=F32
            )
            scale = jnp.sum(jnp.where(lane == at, shrink[...], 0.0), axis=1, keepdims=True)
            raw = (inner[h, rows, :] + carried * start_fade[pl.ds(at, 1), :]) * scale
            square = jnp.mean(raw * raw, axis=1, keepdims=True)
            normed[h, j] = (raw * lax.rsqrt(square + 1e-06) * gain).astype(BF16)
            if i < chunks:
                remote(normed.at[h, j], out_hbm.at[:, target], x_send, x_recv, device).start()
            else:
                pltpu.make_async_copy(normed.at[h, j], out_hbm.at[:, target], own_sem.at[h]).start()

    k_copy.wait()
    v_copy.wait()
    q_copy.start()
    local_state(0)
    pl.semaphore_wait(barrier, ny + nz + chunks - 3)
    for i in range(1, ny):
        remote(end_y.at[my_y], end_y.at[my_y], end_send, end_y_recv, y_peer(i)[1]).start()
    send_y(0)

    @pl.loop(1, DIRECT)
    def _(h):
        local_state(h)
        send_y(h)

    wait_for(end_y.at[pl.ds(0, ny - 1)], end_y_recv)
    group_end = end_y[0]
    for y in range(1, ny):
        group_end = group_end + end_y[y]
    end_z_own[...] = group_end
    end_z[my_z] = group_end
    for i in range(1, nz):
        remote(end_z_own, end_z.at[my_z], end_send, end_z_recv, z_peer(i)[1]).start()
    send_z(0)

    @pl.loop(DIRECT, heads)
    def _(h):
        local_state(h)
        send_y(h)

    z_sent(0)
    send_z(1)

    @pl.loop(DIRECT, heads)
    def _(h):
        group[pl.ds(pl.multiple_of((h - DIRECT) * piece, piece), piece), :] = group_total(h)

    send_group()
    q_copy.wait()
    start_fade[...] = jnp.exp(-start_fade[...])
    shrink[...] = jnp.exp(-grow[...]).T
    grow[...] = jnp.exp(grow[...])
    within(0)
    z_sent(1)
    send_z(2)
    within(1)
    gain_copy.wait()
    wait_for(end_z.at[pl.ds(0, nz - 1)], end_z_recv)
    hand_back(0, direct_before(0))
    z_sent(2)
    send_z(3)
    within(2)
    hand_back(1, direct_before(1))
    finish(0)

    within(3)
    hand_back(2, direct_before(2))
    scan_group()
    finish(1)
    within(4)
    hand_back(3, direct_before(3))
    finish(2)

    wait_for(group_in.at[pl.ds(0, (nz - 1) * share)], gb_recv)

    @pl.loop(DIRECT, heads)
    def _(h):
        hand_back(h, group_before(h))

    @pl.loop(DIRECT, heads)
    def _(h):
        finish(h - 1)

        @pl.when(h + 1 < heads)
        def _():
            within(h + 1)

    finish(heads - 1)

    wait_for(end_y.at[pl.ds(0, ny - 1)], end_send)
    wait_for(end_z.at[pl.ds(0, nz - 1)], end_send)
    wait_for(group_got.at[pl.ds(0, nz - 1)], g_send)
    wait_for(group_got.at[pl.ds(0, nz - 1)], gb_send)

    z_sent(DIRECT - 1)

    @pl.loop(0, heads)
    def _(h):
        wait_for(y_got.at[h, pl.ds(0, ny - 1)], y_send)
        wait_for(back.at[h, pl.ds(0, ny - 1)], b_send)
        wait_for(normed.at[h, pl.ds(0, chunks - 1)], x_send)
        target = pl.ds(pl.multiple_of((head_at * heads + h) * HD, HD), HD)
        pltpu.make_async_copy(normed.at[h, head_at], out_hbm.at[:, target], own_sem.at[h]).wait()

    wait_for(out_hbm.at[:, pl.ds(0, (chunks - 1) * heads * HD)], x_recv)


def on_device(lin_query, lin_key, lin_value, log_decay, norm_gain):
    tokens, width = lin_query.shape
    heads, chunks = width // HD, tokens // CHUNK
    ny = RING_Y
    nz = lax.axis_size("seq") // ny
    piece = HD // ny
    rows = chunks * heads
    share = (heads - DIRECT) * piece // nz
    in_hbm = pl.BlockSpec(memory_space=pltpu.HBM)
    dma = pltpu.SemaphoreType.DMA
    return pl.pallas_call(
        functools.partial(kernel, (heads, chunks, ny, nz)),
        out_shape=pltpu.VMEM((CHUNK, chunks * width), BF16),
        in_specs=[in_hbm] * 5,
        out_specs=pl.BlockSpec(memory_space=pltpu.VMEM),
        scratch_shapes=[
            pltpu.VMEM((tokens, width), BF16),
            pltpu.VMEM((tokens, width), BF16),
            pltpu.VMEM((tokens, width), BF16),
            pltpu.VMEM((heads, tokens), F32),
            pltpu.VMEM((heads, HD), F32),
            pltpu.VMEM((rows, CHUNK), F32),
            pltpu.VMEM((rows, CHUNK), F32),
            pltpu.VMEM((rows, CHUNK), F32),
            pltpu.VMEM((rows, CHUNK), F32),
            pltpu.VMEM((CHUNK, rows), F32),
            pltpu.VMEM((heads, HD, HD), F32),
            pltpu.VMEM((heads, chunks, 2 * HD, HD), BF16),
            pltpu.VMEM((heads, tokens, HD), F32),
            pltpu.VMEM((heads, ny, piece, HD), F32),
            pltpu.VMEM((DIRECT, piece, HD), F32),
            pltpu.VMEM((DIRECT, nz, piece, HD), F32),
            pltpu.VMEM((heads, ny, piece, HD), F32),
            pltpu.VMEM((heads, HD, HD), F32),
            pltpu.VMEM((heads, chunks, CHUNK, HD), BF16),
            pltpu.VMEM((nz * share, HD), F32),
            pltpu.VMEM((nz, share, HD), F32),
            pltpu.VMEM((nz, share, HD), F32),
            pltpu.VMEM((nz * share, HD), F32),
            pltpu.VMEM((ny, heads, HD), F32),
            pltpu.VMEM((heads, HD), F32),
            pltpu.VMEM((nz, heads, HD), F32),
            dma, dma, dma, dma, dma,
            dma, dma, dma, dma, dma((heads,)), dma((DIRECT,)), dma((DIRECT,)), dma, dma((heads,)), dma, dma,
            dma((heads,)), dma, dma, dma, dma,
        ],
        compiler_params=pltpu.CompilerParams(
            collective_id=0, has_side_effects=True, vmem_limit_bytes=60 * 2**20
        ),
        name="lightning",
    )(lin_query, lin_key, lin_value, log_decay.T, norm_gain.reshape(heads, HD))


def solution(mesh):
    in_specs = (P("seq", "head"), P("seq", "head"), P("seq", "head"), P("seq", "head"), P("head"))
    out_specs = P(("seq", "head"), None)
    return jax.shard_map(
        on_device, mesh=mesh, in_specs=in_specs, out_specs=out_specs, check_vma=False
    )
```
